128 devices in a mesh: rows: 32 (over z, x, core), cent: 4 (over y).
Axes of the slice: x: 4, y: 4, z: 4, core: 2. Of those that a mesh axis runs over, the one named last changes fastest.
Arguments:
- embeds: bfloat16 [16384, 768], P('rows'), may hold values from -16 to 16
- centroids: bfloat16 [32768, 768], P('cent'), may hold values from -0.75 to 0.75
Outputs:
- resp: bfloat16 [16384, 32768], P('rows', 'cent')
- weights: float32 [32768], P(('cent', 'rows'))
- numer: float32 [32768, 768], P(('cent', 'rows'))
The draws below stay inside these ranges and needn't reach their ends.
All inputs are finite; a program needn't handle non-finite values.
Results may differ from the reference program's by a relative error of at most 0.01.
Values may be sent and summed in bfloat16 or wider, within the bound.
A program may use at most 128 MiB of HBM per device.

```python
import math
import jax
import jax.numpy as jnp
from jax import lax

D = 768
K = 32768
NROWS = 16384


def shared_centroids(key):
    base = jax.random.normal(key, (K, D), jnp.float32)
    cents = base / jnp.sqrt(D * 1.0)
    cents = jnp.clip(cents, -0.75, 0.75)
    return cents


def draw_centroids(key, part):
    cents = shared_centroids(key)
    return cents.astype(jnp.bfloat16)


def draw_embeds(key, part):
    cents = shared_centroids(key)
    key = jax.random.fold_in(key, 23)
    pick = jax.random.randint(jax.random.fold_in(key, 1), (NROWS,), 0, K)
    noise = jax.random.normal(jax.random.fold_in(key, 2), (NROWS, D), jnp.float32) / jnp.sqrt(D * 1.0)
    rows_out = 0.9 * cents[pick] + 0.45 * noise
    rows_out = jnp.clip(rows_out, -16.0, 16.0)
    return rows_out.astype(jnp.bfloat16)


def setup_inputs(seed: int = 0) -> dict:
    key_of = jax.random.split(jax.random.key(seed), 3)
    embeds = draw_embeds(jax.random.fold_in(key_of[2], 71), 0)
    centroids = draw_centroids(jax.random.fold_in(key_of[2], 71), 0)
    return {"embeds": embeds, "centroids": centroids}


def reference(embeds, centroids):
    block = math.gcd(NROWS, 512)
    count = NROWS // block
    blocks = embeds.reshape(count, block, D)

    def step(carry, rows_block):
        numer_acc, weight_acc = carry
        scores = 10.0 * jnp.dot(rows_block, centroids.T, preferred_element_type=jnp.float32)
        peak = jnp.max(scores, axis=1, keepdims=True)
        expo = jnp.exp(scores - peak)
        total = jnp.sum(expo, axis=1, keepdims=True)
        probs = (expo / total).astype(jnp.bfloat16)
        weight_acc = weight_acc + jnp.sum(probs.astype(jnp.float32), axis=0)
        numer_acc = numer_acc + jnp.dot(probs.T, rows_block, preferred_element_type=jnp.float32)
        return (numer_acc, weight_acc), probs

    init = (jnp.zeros((K, D), jnp.float32), jnp.zeros((K,), jnp.float32))
    (numer, weights), probs = lax.scan(step, init, blocks)
    return probs.reshape(NROWS, K), weights, numer
```

```python
import functools
import math

import jax
import jax.numpy as jnp
from jax import lax
from jax.experimental import pallas as pl
from jax.experimental.pallas import tpu as pltpu
from jax.sharding import PartitionSpec as P

N, D, KL = 512, 768, 8192
NZ = NX = NY = 4
CH = 512
NCH = KL // CH
OWN = 256
DN, QN = 384, 32
DF, QF = 64, 112
SCALE = 10.0 * math.log2(math.e)
F32, BF16 = jnp.float32, jnp.bfloat16
MESH = pl.DeviceIdType.MESH
NT = (((1,), (1,)), ((), ()))
NN = (((1,), (0,)), ((), ()))


def position():
    r = lax.axis_index("rows")
    y = lax.axis_index("cent")
    return lax.div(r, 8), lax.rem(lax.div(r, 2), 4), lax.rem(r, 2), y


def device(dz, dx, dc, dy):
    z, x, c, y = position()
    z, x, y = lax.rem(z + dz, 4), lax.rem(x + dx, 4), lax.rem(y + dy, 4)
    return ((z * 4 + x) * 2 + lax.rem(c + dc, 2), y)


GROUP = [(dx, dc) for dx in range(4) for dc in range(2) if (dx, dc) != (0, 0)]


def slot(dx, dc):
    return dx * 2 + dc


def first_pass(s_ref, m_ref, l_ref):
    for t in range(N // 32):
        rows = pl.ds(t * 32, 32)
        s = [s_ref[rows, pl.ds(g * 128, 128)] for g in range(CH // 128)]
        m = m_ref[rows, :]
        top = functools.reduce(jnp.maximum, s, m)
        total = l_ref[rows, :] * jnp.exp2((m - top) * SCALE)
        for g in s:
            total = total + jnp.exp2((g - top) * SCALE)
        m_ref[rows, :] = top
        l_ref[rows, :] = total


def main_kernel(
    x_hbm, c_hbm, own_ref, w_ref, p1_ref, p2_ref, p3_ref, stat_ref,
    xg, cv, s0, s1, m_ref, l_ref, acc, cols, stats, ystats,
    load_sem, c_sem, gs, gr, ys, yr, ss, sr,
):
    z, x, c, y = position()
    bar = pltpu.get_barrier_semaphore()
    peers = [(0, dx, dc, 0) for dx, dc in GROUP] + [(0, 0, 0, dy) for dy in (1, 2, 3)]
    for p in peers:
        pl.semaphore_signal(bar, inc=1, device_id=device(*p), device_id_type=MESH)
    load = pltpu.make_async_copy(x_hbm, xg.at[0], load_sem)
    load.start()

    def c_copy(j):
        return pltpu.make_async_copy(c_hbm.at[pl.ds(j * CH, CH)], cv.at[j], c_sem.at[j])

    @pl.loop(0, NCH)
    def _(j):
        c_copy(j).start()

    m_ref[...] = jnp.full(m_ref.shape, -3e38, F32)
    l_ref[...] = jnp.zeros(l_ref.shape, F32)
    acc[...] = jnp.zeros(acc.shape, F32)
    cols[...] = jnp.zeros(cols.shape, F32)
    load.wait()

    def scores(j, out):
        out[...] = lax.dot_general(xg[0], cv[j], NT, preferred_element_type=F32)

    c_copy(0).wait()
    scores(0, s0)

    def steps(a, b):
        @pl.loop(a, b)
        def _(i):
            c_copy(2 * i + 1).wait()
            c_copy(2 * i + 2).wait()
            scores(2 * i + 1, s1)
            first_pass(s0, m_ref, l_ref)
            scores(2 * i + 2, s0)
            first_pass(s1, m_ref, l_ref)

    def remote(src, dst, send, recv, to):
        return pltpu.make_async_remote_copy(
            src_ref=src, dst_ref=dst, send_sem=send, recv_sem=recv, device_id=device(*to), device_id_type=MESH
        )

    def piece(s, rows, k, to, lands=None):
        lands = s if lands is None else lands
        return remote(xg.at[s, rows], xg.at[lands, rows], gs.at[k], gr.at[k], to)

    def quarter(s, q):
        d, n = (DF, QF) if s == 4 else (DN, QN)
        return pl.ds(pl.multiple_of(d + n * q, 16), n)

    def direct(s):
        return pl.ds(0, DF if s == 4 else DN)

    def shared(s):
        d = DF if s == 4 else DN
        return pl.ds(d, N - d)

    sibling = piece(0, pl.ds(0, N), 0, (0, 0, 1, 0), 1)
    x_shared = {s: piece(0, quarter(s, y), 1 + i, (0, 4 - s // 2, 0, 0), s) for i, s in enumerate((4, 2, 6))}
    x_direct = {s: piece(0, direct(s), 4 + i, (0, 4 - s // 2, 0, 0), s) for i, s in enumerate((2, 6, 4))}

    def y_send(s, dy):
        k = (s // 2 - 1) * 3 + dy - 1
        return remote(xg.at[s, quarter(s, y)], xg.at[s, quarter(s, y)], ys.at[k], yr.at[k], (0, 0, 0, dy))

    def y_recv(s, dy):
        k = (s // 2 - 1) * 3 + dy - 1
        q = quarter(s, lax.rem(y + 4 - dy, 4))
        return remote(xg.at[s, q], xg.at[s, q], ys.at[k], yr.at[k], (0, 0, 0, dy))

    pass_direct = {s: piece(s, direct(s), 7 + i, (0, 0, 1, 0), s + 1) for i, s in enumerate((2, 6, 4))}
    pass_shared = {s: piece(s, shared(s), 10 + i, (0, 0, 1, 0), s + 1) for i, s in enumerate((2, 6, 4))}

    def stat_copy(dx, dc):
        k = slot((4 - dx) % 4, dc)
        return remote(stats.at[0], stats.at[k], ss.at[k], sr.at[k], (0, dx, dc, 0))

    def ystat_copy(dy):
        return remote(ystats.at[0], ystats.at[dy], ss.at[7 + dy], sr.at[7 + dy], (0, 0, 0, dy))

    steps(0, 2)
    pl.semaphore_wait(bar, len(peers))
    for s in (4, 2, 6):
        x_shared[s].start()
    sibling.start()
    steps(2, 5)
    for s in (2, 6, 4):
        x_direct[s].start()
    steps(5, 7)
    c_copy(NCH - 1).wait()
    scores(NCH - 1, s1)
    first_pass(s0, m_ref, l_ref)
    first_pass(s1, m_ref, l_ref)

    m_t = jnp.transpose(m_ref[...])
    l_t = jnp.transpose(l_ref[...])
    top = jnp.max(m_t, axis=0, keepdims=True)
    total = jnp.sum(l_t * jnp.exp2((m_t - top) * SCALE), axis=0, keepdims=True)
    ystats[0, 0:8, :] = jnp.broadcast_to(top, (8, N))
    ystats[0, 8:16, :] = jnp.broadcast_to(total, (8, N))
    for dy in (1, 2, 3):
        ystat_copy(dy).start()
    for s in (2, 6, 4):
        x_shared[s].wait_recv()
        for dy in (1, 3, 2):
            y_send(s, dy).start()
    for dy in (1, 2, 3):
        ystat_copy(dy).wait_recv()
    tops = [ystats[dy, 0:8, :] for dy in range(4)]
    top = functools.reduce(jnp.maximum, tops)
    total = sum(ystats[dy, 8:16, :] * jnp.exp2((tops[dy] - top) * SCALE) for dy in range(4))
    stats[0, 0:8, :] = top
    stats[0, 8:16, :] = 1.0 / total
    stat_ref[0:8, :] = top
    stat_ref[8:16, :] = 1.0 / total
    for dx, dc in GROUP:
        stat_copy(dx, dc).start()

    def group(dx, dc):
        k = slot(dx, dc)
        rows = xg[k]
        top = stats[k, 0:1, :]
        inv = stats[k, 8:9, :]
        for q in range(4):
            block = lax.rem(z + q, 4) * 8 + x * 2 + c
            half = lax.rem(block, 2) * OWN
            cents = cv[lax.div(block, 2), pl.ds(pl.multiple_of(half, OWN), OWN), :]
            s = lax.dot_general(cents, rows, NT, preferred_element_type=F32)
            p = (jnp.exp2((s - top) * SCALE) * inv).astype(BF16)
            w = p.astype(F32)
            cols[q] += sum(w[:, g * 128 : (g + 1) * 128] for g in range(N // 128))
            acc[q] += lax.dot_general(p, rows, NN, preferred_element_type=F32)

    group(0, 0)
    sibling.wait_recv()
    stat_copy(0, 1).wait_recv()
    group(0, 1)
    for dx in (1, 3, 2):
        s = 2 * dx
        x_direct[s].wait_recv()
        pass_direct[s].start()
        for dy in (1, 3, 2):
            y_recv(s, dy).wait_recv()
        pass_shared[s].start()
        for dc in range(2):
            stat_copy((4 - dx) % 4, dc).wait_recv()
        group(dx, 0)
        pass_direct[s].wait_recv()
        pass_shared[s].wait_recv()
        group(dx, 1)

    own_ref[...] = acc[0]
    for q, out in enumerate((None, p1_ref, p2_ref, p3_ref)):
        w = jnp.sum(jnp.transpose(cols[q]), axis=0, keepdims=True)
        if q == 0:
            w_ref[...] = jnp.broadcast_to(w, (8, OWN))
            continue
        out[0:OWN, :] = acc[q].astype(BF16)
        high = w.astype(BF16)
        low = (w - high.astype(F32)).astype(BF16)
        tail = jnp.concatenate([high.astype(F32), low.astype(F32), jnp.zeros((1, OWN), F32)], axis=1)
        out[OWN : OWN + 16, :] = jnp.broadcast_to(tail, (16, D)).astype(BF16)

    sibling.wait_send()
    for s in (2, 6, 4):
        for copy in (x_shared[s], x_direct[s], pass_direct[s], pass_shared[s]):
            copy.wait_send()
        for dy in (1, 2, 3):
            y_send(s, dy).wait_send()
    for dy in (1, 2, 3):
        ystat_copy(dy).wait_send()
    for dx, dc in GROUP:
        stat_copy(dx, dc).wait_send()


def main_call(embeds, centroids):
    part = jax.ShapeDtypeStruct((OWN + 16, D), BF16)
    vmem = pl.BlockSpec(memory_space=pltpu.VMEM)
    dma = pltpu.SemaphoreType.DMA
    return pl.pallas_call(
        main_kernel,
        out_shape=[
            jax.ShapeDtypeStruct((OWN, D), F32),
            jax.ShapeDtypeStruct((8, OWN), F32),
            part, part, part,
            jax.ShapeDtypeStruct((16, N), F32),
        ],
        in_specs=[pl.BlockSpec(memory_space=pl.ANY)] * 2,
        out_specs=[vmem] * 6,
        scratch_shapes=[
            pltpu.VMEM((8, N, D), BF16),
            pltpu.VMEM((NCH, CH, D), BF16),
            pltpu.VMEM((N, CH), F32),
            pltpu.VMEM((N, CH), F32),
            pltpu.VMEM((N, 128), F32),
            pltpu.VMEM((N, 128), F32),
            pltpu.VMEM((4, OWN, D), F32),
            pltpu.VMEM((4, OWN, 128), F32),
            pltpu.VMEM((8, 16, N), F32),
            pltpu.VMEM((4, 16, N), F32),
            dma(()), dma((NCH,)), dma((13,)), dma((13,)), dma((9,)), dma((9,)), dma((11,)), dma((11,)),
        ],
        compiler_params=pltpu.CompilerParams(
            collective_id=0, has_side_effects=True, vmem_limit_bytes=48 << 20
        ),
        cost_estimate=pl.CostEstimate(flops=20_000_000_000, bytes_accessed=20_000_000, transcendentals=8_000_000),
    )(embeds, centroids)


RC = 1024


def resp_kernel(stat_ref, x_ref, c_ref, out_ref, top, inv):
    @pl.when(pl.program_id(0) == 0)
    def _():
        top[...] = jnp.transpose(jnp.broadcast_to(stat_ref[0:1, :], (128, N)))
        inv[...] = jnp.transpose(jnp.broadcast_to(stat_ref[8:9, :], (128, N)))

    for h in range(RC // 256):
        s = lax.dot_general(x_ref[...], c_ref[pl.ds(h * 256, 256), :], NT, preferred_element_type=F32)
        for g in range(2):
            t = s[:, g * 128 : (g + 1) * 128]
            out_ref[:, pl.ds(h * 256 + g * 128, 128)] = (jnp.exp2((t - top[...]) * SCALE) * inv[...]).astype(BF16)


def resp_call(stat, embeds, centroids):
    return pl.pallas_call(
        resp_kernel,
        out_shape=jax.ShapeDtypeStruct((N, KL), BF16),
        grid=(KL // RC,),
        in_specs=[
            pl.BlockSpec((16, N), lambda j: (0, 0)),
            pl.BlockSpec((N, D), lambda j: (0, 0)),
            pl.BlockSpec((RC, D), lambda j: (j, 0)),
        ],
        out_specs=pl.BlockSpec((N, RC), lambda j: (0, j)),
        scratch_shapes=[pltpu.VMEM((N, 128), F32), pltpu.VMEM((N, 128), F32)],
        compiler_params=pltpu.CompilerParams(vmem_limit_bytes=32 << 20),
        cost_estimate=pl.CostEstimate(flops=6_500_000_000, bytes_accessed=22_000_000, transcendentals=4_200_000),
    )(stat, embeds, centroids)


def sum_kernel(own_ref, w_ref, a_ref, b_ref, c_ref, numer_ref, weight_ref):
    parts = (a_ref, b_ref, c_ref)
    numer_ref[...] = own_ref[...] + sum(p[0:OWN, :].astype(F32) for p in parts)
    w = w_ref[...]
    for p in parts:
        tail = p[OWN : OWN + 16, :].astype(F32)
        w = w + tail[0:8, 0:OWN] + tail[0:8, OWN : 2 * OWN]
    weight_ref[...] = w


def sum_call(own, w, a, b, c):
    return pl.pallas_call(
        sum_kernel,
        out_shape=[jax.ShapeDtypeStruct((OWN, D), F32), jax.ShapeDtypeStruct((8, OWN), F32)],
    )(own, w, a, b, c)


def along_z(part, dz):
    perm = [(r, (r + 8 * dz) % 32) for r in range(32)]
    return lax.ppermute(part, "rows", perm)


def shards(embeds, centroids):
    own, w, p1, p2, p3, stat = main_call(embeds, centroids)
    got = [along_z(p, dz) for p, dz in ((p2, 2), (p1, 1), (p3, 3))]
    resp = resp_call(stat, embeds, centroids)
    numer, weights = sum_call(own, w, *got)
    return resp, weights[0], numer


def solution(mesh):
    return jax.shard_map(
        shards,
        mesh=mesh,
        in_specs=(P("rows", None), P("cent", None)),
        out_specs=(P("rows", "cent"), P(("cent", "rows")), P(("cent", "rows"), None)),
        check_vma=False,
    )
```

```python
import functools
import math

import jax
import jax.numpy as jnp
from jax import lax
from jax.experimental import pallas as pl
from jax.experimental.pallas import tpu as pltpu
from jax.sharding import PartitionSpec as P

N, D, KL = 512, 768, 8192
NZ = NX = NY = 4
CH = 512
AHEAD = 6
NCH = KL // CH
OWN = 256
QF = 128
PIECE = 128
HALF = 128
PART = HALF + 16
VMEM_LIMIT = 40 << 20
SCALE = 10.0 * math.log2(math.e)
F32, BF16 = jnp.float32, jnp.bfloat16
MESH = pl.DeviceIdType.MESH
NT = (((1,), (1,)), ((), ()))
NN = (((1,), (0,)), ((), ()))


def position():
    r = lax.axis_index("rows")
    y = lax.axis_index("cent")
    return lax.div(r, 8), lax.rem(lax.div(r, 2), 4), lax.rem(r, 2), y


def device(dz, dx, dc, dy):
    z, x, c, y = position()
    z, x, y = lax.rem(z + dz, 4), lax.rem(x + dx, 4), lax.rem(y + dy, 4)
    return ((z * 4 + x) * 2 + lax.rem(c + dc, 2), y)


def first_pass(s_ref, m_ref, l_ref):
    for t in range(N // 32):
        rows = pl.ds(t * 32, 32)
        s = [s_ref[rows, pl.ds(g * 128, 128)] for g in range(CH // 128)]
        m = m_ref[rows, :]
        top = functools.reduce(jnp.maximum, s, m)
        total = l_ref[rows, :] * jnp.exp2((m - top) * SCALE)
        for g in s:
            total = total + jnp.exp2((g - top) * SCALE)
        m_ref[rows, :] = top
        l_ref[rows, :] = total


def slot(h, d, dc):
    return d * 2 + dc + 6 * h if d else dc


def to_axis(h, d, dc=0):
    return (0, d, dc, 0) if h == 0 else (d, 0, dc, 0)


PEERS = [(0, 0, 1, 0)] + [to_axis(h, d, dc) for h in range(2) for d in (1, 2, 3) for dc in range(2)]
YPEERS = [(0, 0, 0, dy) for dy in (1, 2, 3)]


def main_kernel(
    x_ref, c_hbm, resp_ref, numer_ref, w_ref,
    xs, xn, xf, cv, cc, s0, s1, m_ref, l_ref, acc, cols, stats, ystats, topc, invc, sb, rb,
    c_sem, cc_sem, own_s, own_r, near_s, near_r, far_s, far_r, ys, yr, pn_s, pn_r, pf_s, pf_r, ss, sr, yss, ysr, rs, rr,
):
    z, x, c, y = position()
    def c_copy(j):
        return pltpu.make_async_copy(c_hbm.at[pl.ds(j * CH, CH)], cv.at[j], c_sem.at[j])

    def cc_copy(h, q):
        owner = lax.rem(z + q, 4) * 8 + x * 2 + c if h == 0 else z * 8 + lax.rem(x + q, 4) * 2 + c
        start = pl.multiple_of(owner * OWN + h * HALF, HALF)
        return pltpu.make_async_copy(
            c_hbm.at[pl.ds(start, HALF)], cc.at[h, pl.ds(q * HALF, HALF)], cc_sem.at[h, q]
        )

    for j in range(AHEAD):
        c_copy(j).start()
    bar = pltpu.get_barrier_semaphore()
    for p in PEERS + YPEERS:
        pl.semaphore_signal(bar, inc=1, device_id=device(*p), device_id_type=MESH)
    m_ref[...] = jnp.full(m_ref.shape, -3e38, F32)
    l_ref[...] = jnp.zeros(l_ref.shape, F32)
    acc[...] = jnp.zeros(acc.shape, F32)
    cols[...] = jnp.zeros(cols.shape, F32)

    def scores(j, out):
        out[...] = lax.dot_general(x_ref[...], cv[j], NT, preferred_element_type=F32)

    c_copy(0).wait()
    scores(0, s0)

    def steps(a, b):
        @pl.loop(a, b)
        def _(i):
            c_copy(2 * i + 1).wait()
            c_copy(2 * i + 2).wait()
            scores(2 * i + 1, s1)
            first_pass(s0, m_ref, l_ref)
            scores(2 * i + 2, s0)
            first_pass(s1, m_ref, l_ref)

            @pl.when(i < (NCH - AHEAD) // 2)
            def _():
                c_copy(2 * i + AHEAD).start()
                c_copy(2 * i + AHEAD + 1).start()

    def remote(src, dst, send, recv, to):
        return pltpu.make_async_remote_copy(
            src_ref=src, dst_ref=dst, send_sem=send, recv_sem=recv, device_id=device(*to), device_id_type=MESH
        )

    sibling = remote(x_ref, xs, own_s, own_r, (0, 0, 1, 0))

    def near(h, k, side):
        rows = pl.ds(side * PIECE, PIECE)
        return remote(
            x_ref.at[pl.ds(k * PIECE, PIECE)], xn.at[h, k, rows],
            near_s.at[h, k, side], near_r.at[h, k, side], to_axis(h, 3 if side == 0 else 1),
        )

    def pass_near(h, k):
        return remote(
            xn.at[h, k, pl.ds(0, 2 * PIECE)], xn.at[h, k, pl.ds(2 * PIECE, 2 * PIECE)],
            pn_s.at[h, k], pn_r.at[h, k], (0, 0, 1, 0),
        )

    def quarter(q):
        return pl.ds(pl.multiple_of(QF * q, QF), QF)

    def far(h):
        rows = quarter(y)
        return remote(x_ref.at[rows], xf.at[h, 0, rows], far_s.at[h], far_r.at[h], to_axis(h, 2))

    def y_send(h, dy):
        rows = xf.at[h, 0, quarter(y)]
        return remote(rows, rows, ys.at[h, dy], yr.at[h, dy], (0, 0, 0, dy))

    def y_recv(h, dy):
        rows = xf.at[h, 0, quarter(lax.rem(y + 4 - dy, 4))]
        return remote(rows, rows, ys.at[h, dy], yr.at[h, dy], (0, 0, 0, dy))

    def pass_far(h, dy):
        rows = quarter(lax.rem(y + 4 - dy, 4))
        return remote(xf.at[h, 0, rows], xf.at[h, 1, rows], pf_s.at[h, dy], pf_r.at[h, dy], (0, 0, 1, 0))

    def stat_copy(h, d, dc):
        k = slot(h, d, dc)
        to = to_axis(h, (4 - d) % 4, dc)
        return remote(stats.at[0], stats.at[k], ss.at[k], sr.at[k], to)

    def ystat_copy(dy):
        return remote(ystats.at[0], ystats.at[dy], yss.at[dy], ysr.at[dy], (0, 0, 0, dy))

    def start_near(k):
        for side in range(2):
            for h in range(2):
                near(h, k, side).start()

    def take_near(k):
        for h in range(2):
            for side in range(2):
                near(h, k, side).wait_recv()
            pass_near(h, k).start()

    steps(0, 2)
    pl.semaphore_wait(bar, len(PEERS) + len(YPEERS))
    for h in range(2):
        far(h).start()
    sibling.start()
    steps(2, 4)
    start_near(0)
    for h in range(2):
        for q in range(4):
            cc_copy(h, q).start()
    steps(4, 6)
    start_near(1)
    steps(6, 7)
    c_copy(NCH - 1).wait()
    scores(NCH - 1, s1)
    first_pass(s0, m_ref, l_ref)
    first_pass(s1, m_ref, l_ref)

    m_t = jnp.transpose(m_ref[...])
    l_t = jnp.transpose(l_ref[...])
    top = jnp.max(m_t, axis=0, keepdims=True)
    total = jnp.sum(l_t * jnp.exp2((m_t - top) * SCALE), axis=0, keepdims=True)
    ystats[0, 0:8, :] = jnp.broadcast_to(top, (8, N))
    ystats[0, 8:16, :] = jnp.broadcast_to(total, (8, N))
    for dy in (1, 2, 3):
        ystat_copy(dy).start()
    for h in range(2):
        far(h).wait_recv()
        if h == 0:
            for dy in (1, 3, 2):
                y_send(h, dy).start()
        pass_far(h, 0).start()
    start_near(2)
    for dy in (1, 2, 3):
        ystat_copy(dy).wait_recv()
    tops = [ystats[dy, 0:8, :] for dy in range(4)]
    top = functools.reduce(jnp.maximum, tops)
    total = sum(ystats[dy, 8:16, :] * jnp.exp2((tops[dy] - top) * SCALE) for dy in range(4))
    inv = 1.0 / total
    stats[0, 0:8, :] = top
    stats[0, 8:16, :] = inv
    stat_copy(0, 0, 1).start()
    for d in (1, 3, 2):
        for h in range(2):
            for dc in range(2):
                stat_copy(h, d, dc).start()

    def sums(h, rows_ref, top, inv):
        rows = rows_ref[...]
        for u in range(2):
            span = pl.ds(u * 256, 256)
            s = lax.dot_general(cc[h, span, :], rows, NT, preferred_element_type=F32)
            p = (jnp.exp2((s - top) * SCALE) * inv).astype(BF16)
            w = p.astype(F32)
            cols[h, span, :] += sum(w[:, g * 128 : (g + 1) * 128] for g in range(N // 128))
            acc[h, span, :] += lax.dot_general(p, rows, NN, preferred_element_type=F32)

    def chip_sums(rows, k):
        for h in range(2):
            sums(h, rows, stats[k, 0:1, :], stats[k, 8:9, :])

    def near_sums(k):
        for h in range(2):
            pass_near(h, k).wait_recv()
        lanes = pl.ds(k * PIECE, PIECE)
        for h in range(2):
            order = [slot(h, d, dc) for dc in range(2) for d in (1, 3)]
            top = jnp.concatenate([stats[i, 0:1, lanes] for i in order], axis=1)
            inv = jnp.concatenate([stats[i, 8:9, lanes] for i in order], axis=1)
            sums(h, xn.at[h, k], top, inv)

    def far_sums(h):
        for dy in range(4):
            pass_far(h, dy).wait_recv()
        for dc in range(2):
            k = slot(h, 2, dc)
            sums(h, xf.at[h, dc], stats[k, 0:1, :], stats[k, 8:9, :])

    def take_far(h, dy):
        y_recv(h, dy).wait_recv()
        pass_far(h, dy).start()

    def part(h, q):
        return remote(sb.at[h, q], rb.at[h, q], rs.at[h, q], rr.at[h, q], to_axis(1 - h, q))

    def tail(h, q):
        return jnp.sum(jnp.transpose(cols[h, pl.ds(q * HALF, HALF), :]), axis=0, keepdims=True)

    def send_parts(h):
        for q in (2, 1, 3):
            sb[h, q, 0:HALF, :] = acc[h, pl.ds(q * HALF, HALF), :].astype(BF16)
            w = tail(h, q)
            high = w.astype(BF16).astype(F32)
            row = jnp.concatenate([high, w - high, jnp.zeros((1, D - 2 * HALF), F32)], axis=1)
            sb[h, q, HALF:PART, :] = jnp.broadcast_to(row, (16, D)).astype(BF16)
            part(h, q).start()

    def resp(a, b):
        @pl.loop(a, b)
        def _(j):
            for u in range(2):
                s = lax.dot_general(x_ref[...], cv[j, pl.ds(u * 256, 256), :], NT, preferred_element_type=F32)
                for g in range(2):
                    t = s[:, g * 128 : (g + 1) * 128]
                    lanes = pl.ds(pl.multiple_of(j * CH + u * 256 + g * 128, 128), 128)
                    resp_ref[:, lanes] = (jnp.exp2((t - topc[...]) * SCALE) * invc[...]).astype(BF16)

    take_near(0)
    for h in range(2):
        for q in range(4):
            cc_copy(h, q).wait()
    chip_sums(x_ref, 0)
    for dy in (1, 3, 2):
        y_send(1, dy).start()
    sibling.wait_recv()
    stat_copy(0, 0, 1).wait_recv()
    chip_sums(xs, 1)
    take_near(1)
    start_near(3)
    for h in range(2):
        for d in (1, 2, 3):
            for dc in range(2):
                stat_copy(h, d, dc).wait_recv()
    near_sums(0)
    take_near(2)
    near_sums(1)
    for dy in (1, 3, 2):
        take_far(0, dy)
    near_sums(2)
    take_near(3)
    far_sums(0)
    take_far(1, 1)
    take_far(1, 3)
    near_sums(3)
    send_parts(0)
    take_far(1, 2)
    topc[...] = jnp.transpose(jnp.broadcast_to(stats[0, 0:1, :], (128, N)))
    invc[...] = jnp.transpose(jnp.broadcast_to(stats[0, 8:9, :], (128, N)))
    far_sums(1)
    send_parts(1)
    resp(0, NCH)

    for h in (0, 1):
        total = acc[h, 0:HALF, :]
        w = tail(h, 0)
        for q in (1, 3, 2):
            part(h, q).wait_recv()
            total = total + rb[h, q, 0:HALF, :].astype(F32)
            row = rb[h, q, HALF:PART, :].astype(F32)[0:1, :]
            w = w + row[:, 0:HALF] + row[:, HALF : 2 * HALF]
        numer_ref[pl.ds(h * HALF, HALF), :] = total
        w_ref[:, pl.ds(h * HALF, HALF)] = jnp.broadcast_to(w, (8, HALF))

    sibling.wait_send()
    stat_copy(0, 0, 1).wait_send()
    for h in range(2):
        far(h).wait_send()
        for k in range(4):
            pass_far(h, k).wait_send()
            pass_near(h, k).wait_send()
            for side in range(2):
                near(h, k, side).wait_send()
        for d in (1, 2, 3):
            y_send(h, d).wait_send()
            part(h, d).wait_send()
            for dc in range(2):
                stat_copy(h, d, dc).wait_send()
    for dy in (1, 2, 3):
        ystat_copy(dy).wait_send()


def main_call(embeds, centroids):
    vmem = pl.BlockSpec(memory_space=pltpu.VMEM)
    dma = pltpu.SemaphoreType.DMA
    return pl.pallas_call(
        main_kernel,
        out_shape=[
            jax.ShapeDtypeStruct((N, KL), BF16),
            jax.ShapeDtypeStruct((OWN, D), F32),
            jax.ShapeDtypeStruct((8, OWN), F32),
        ],
        in_specs=[vmem, pl.BlockSpec(memory_space=pl.ANY)],
        out_specs=[vmem] * 3,
        scratch_shapes=[
            pltpu.VMEM((N, D), BF16),
            pltpu.VMEM((2, 4, 4 * PIECE, D), BF16),
            pltpu.VMEM((2, 2, N, D), BF16),
            pltpu.VMEM((NCH, CH, D), BF16),
            pltpu.VMEM((2, 4 * HALF, D), BF16),
            pltpu.VMEM((N, CH), F32),
            pltpu.VMEM((N, CH), F32),
            pltpu.VMEM((N, 128), F32),
            pltpu.VMEM((N, 128), F32),
            pltpu.VMEM((2, 4 * HALF, D), F32),
            pltpu.VMEM((2, 4 * HALF, 128), F32),
            pltpu.VMEM((14, 16, N), F32),
            pltpu.VMEM((4, 16, N), F32),
            pltpu.VMEM((N, 128), F32),
            pltpu.VMEM((N, 128), F32),
            pltpu.VMEM((2, 4, PART, D), BF16),
            pltpu.VMEM((2, 4, PART, D), BF16),
            dma((NCH,)), dma((2, 4)), dma(()), dma(()),
            dma((2, 4, 2)), dma((2, 4, 2)), dma((2,)), dma((2,)), dma((2, 4)), dma((2, 4)),
            dma((2, 4)), dma((2, 4)), dma((2, 4)), dma((2, 4)), dma((14,)), dma((14,)), dma((4,)), dma((4,)),
            dma((2, 4)), dma((2, 4)),
        ],
        compiler_params=pltpu.CompilerParams(
            collective_id=0, has_side_effects=True, vmem_limit_bytes=VMEM_LIMIT
        ),
        cost_estimate=pl.CostEstimate(flops=26_000_000_000, bytes_accessed=22_000_000, transcendentals=13_000_000),
    )(embeds, centroids)


def out_kernel(resp_ref, numer_ref, w_ref, resp_out, numer_out, w_out, sem):
    copies = [
        pltpu.make_async_copy(resp_ref.at[pl.ds(i * 64, 64)], resp_out.at[pl.ds(i * 64, 64)], sem.at[i])
        for i in range(8)
    ]
    copies.append(pltpu.make_async_copy(numer_ref, numer_out, sem.at[8]))
    for copy in copies:
        copy.start()
    w_out[...] = w_ref[0:1, :]
    for copy in copies:
        copy.wait()


def out_call(resp, numer, weights):
    vmem, any_ = pl.BlockSpec(memory_space=pltpu.VMEM), pl.BlockSpec(memory_space=pl.ANY)
    return pl.pallas_call(
        out_kernel,
        out_shape=[
            jax.ShapeDtypeStruct((N, KL), BF16),
            jax.ShapeDtypeStruct((OWN, D), F32),
            jax.ShapeDtypeStruct((1, OWN), F32),
        ],
        in_specs=[vmem] * 3,
        out_specs=[any_, any_, vmem],
        scratch_shapes=[pltpu.SemaphoreType.DMA((9,))],
        compiler_params=pltpu.CompilerParams(vmem_limit_bytes=20 << 20),
    )(resp, numer, weights)


def shards(embeds, centroids):
    resp, numer, weights = out_call(*main_call(embeds, centroids))
    return resp, jnp.reshape(weights, (OWN,)), numer


def solution(mesh):
    return jax.shard_map(
        shards,
        mesh=mesh,
        in_specs=(P("rows", None), P("cent", None)),
        out_specs=(P("rows", "cent"), P(("cent", "rows")), P(("cent", "rows"), None)),
        check_vma=False,
    )
```

```python
import functools
import math

import jax
import jax.numpy as jnp
from jax import lax
from jax.experimental import pallas as pl
from jax.experimental.pallas import tpu as pltpu
from jax.sharding import PartitionSpec as P

N, D, KL = 512, 768, 8192
NZ = NX = NY = 4
CH = 512
AHEAD = 6
NCH = KL // CH
OWN = 256
QF = 128
PIECE = 256
HALF = 128
VMEM_LIMIT = 40 << 20
SCALE = 10.0 * math.log2(math.e)
F32, BF16 = jnp.float32, jnp.bfloat16
MESH = pl.DeviceIdType.MESH
NT = (((1,), (1,)), ((), ()))
NN = (((1,), (0,)), ((), ()))


def position():
    r = lax.axis_index("rows")
    y = lax.axis_index("cent")
    return lax.div(r, 8), lax.rem(lax.div(r, 2), 4), lax.rem(r, 2), y


def device(dz, dx, dc, dy):
    z, x, c, y = position()
    z, x, y = lax.rem(z + dz, 4), lax.rem(x + dx, 4), lax.rem(y + dy, 4)
    return ((z * 4 + x) * 2 + lax.rem(c + dc, 2), y)


def first_pass(s_ref, m_ref, l_ref):
    for t in range(N // 32):
        rows = pl.ds(t * 32, 32)
        s = [s_ref[rows, pl.ds(g * 128, 128)] for g in range(CH // 128)]
        m = m_ref[rows, :]
        top = functools.reduce(jnp.maximum, s, m)
        total = l_ref[rows, :] * jnp.exp2((m - top) * SCALE)
        for g in s:
            total = total + jnp.exp2((g - top) * SCALE)
        m_ref[rows, :] = top
        l_ref[rows, :] = total


def slot(h, d):
    return d + 3 * h if d else 0


def to_axis(h, d, dc=0):
    return (0, d, dc, 0) if h == 0 else (d, 0, dc, 0)


PEERS = [(0, 0, 1, 0)] + [to_axis(h, d, dc) for h in range(2) for d in (1, 2, 3) for dc in range(2)]
YPEERS = [(0, 0, 0, dy) for dy in (1, 2, 3)]


def main_kernel(
    x_ref, c_hbm, resp_ref, numer_ref, w_ref,
    xs, xn, xf, cv, cc, s0, s1, m_ref, l_ref, acc, cols, stats, ystats, topc, invc, sb, rb, wsb, wrb,
    c_sem, cc_sem, own_s, own_r, near_s, near_r, far_s, far_r, ys, yr, pn_s, pn_r, pf_s, pf_r, ss, sr, yss, ysr, rs, rr, ws, wr,
):
    z, x, c, y = position()
    def c_copy(j):
        return pltpu.make_async_copy(c_hbm.at[pl.ds(j * CH, CH)], cv.at[j], c_sem.at[j])

    def cc_copy(h, q):
        owner = lax.rem(z + q, 4) * 8 + x * 2 + c if h == 0 else z * 8 + lax.rem(x + q, 4) * 2 + c
        start = pl.multiple_of(owner * OWN + h * HALF, HALF)
        return pltpu.make_async_copy(
            c_hbm.at[pl.ds(start, HALF)], cc.at[h, pl.ds(q * HALF, HALF)], cc_sem.at[h, q]
        )

    for j in range(AHEAD):
        c_copy(j).start()
    bar = pltpu.get_barrier_semaphore()
    for p in PEERS + YPEERS:
        pl.semaphore_signal(bar, inc=1, device_id=device(*p), device_id_type=MESH)
    m_ref[...] = jnp.full(m_ref.shape, -3e38, F32)
    l_ref[...] = jnp.zeros(l_ref.shape, F32)
    acc[...] = jnp.zeros(acc.shape, F32)
    cols[...] = jnp.zeros(cols.shape, F32)

    def scores(j, out):
        out[...] = lax.dot_general(x_ref[...], cv[j], NT, preferred_element_type=F32)

    c_copy(0).wait()
    scores(0, s0)

    def steps(a, b):
        @pl.loop(a, b)
        def _(i):
            c_copy(2 * i + 1).wait()
            c_copy(2 * i + 2).wait()
            scores(2 * i + 1, s1)
            first_pass(s0, m_ref, l_ref)
            scores(2 * i + 2, s0)
            first_pass(s1, m_ref, l_ref)

            @pl.when(i < (NCH - AHEAD) // 2)
            def _():
                c_copy(2 * i + AHEAD).start()
                c_copy(2 * i + AHEAD + 1).start()

    def remote(src, dst, send, recv, to):
        return pltpu.make_async_remote_copy(
            src_ref=src, dst_ref=dst, send_sem=send, recv_sem=recv, device_id=device(*to), device_id_type=MESH
        )

    sibling = remote(x_ref, xs, own_s, own_r, (0, 0, 1, 0))

    def near(h, k, side):
        rows = pl.ds(side * PIECE, PIECE)
        return remote(
            x_ref.at[pl.ds(k * PIECE, PIECE)], xn.at[h, k, rows],
            near_s.at[h, k, side], near_r.at[h, k, side], to_axis(h, 3 if side == 0 else 1),
        )

    def pass_near(h, k):
        return remote(
            xn.at[h, k, pl.ds(0, 2 * PIECE)], xn.at[h, k, pl.ds(2 * PIECE, 2 * PIECE)],
            pn_s.at[h, k], pn_r.at[h, k], (0, 0, 1, 0),
        )

    def quarter(q):
        return pl.ds(pl.multiple_of(QF * q, QF), QF)

    def far(h):
        rows = quarter(y)
        return remote(x_ref.at[rows], xf.at[h, 0, rows], far_s.at[h], far_r.at[h], to_axis(h, 2))

    def y_send(h, dy):
        rows = xf.at[h, 0, quarter(y)]
        return remote(rows, rows, ys.at[h, dy], yr.at[h, dy], (0, 0, 0, dy))

    def y_recv(h, dy):
        rows = xf.at[h, 0, quarter(lax.rem(y + 4 - dy, 4))]
        return remote(rows, rows, ys.at[h, dy], yr.at[h, dy], (0, 0, 0, dy))

    def pass_far(h):
        return remote(xf.at[h, 0], xf.at[h, 1], pf_s.at[h], pf_r.at[h], (0, 0, 1, 0))

    def stat_copy(h, d):
        k = slot(h, d)
        return remote(stats.at[0, 0], stats.at[0, k], ss.at[k], sr.at[k], to_axis(h, 4 - d))

    def stat_sibling():
        return remote(stats.at[0, 0], stats.at[1, 0], ss.at[0], sr.at[0], (0, 0, 1, 0))

    def stat_pass():
        rows = pl.ds(1, 6)
        return remote(stats.at[0, rows], stats.at[1, rows], ss.at[7], sr.at[7], (0, 0, 1, 0))

    def ystat_copy(dy):
        return remote(ystats.at[0], ystats.at[dy], yss.at[dy], ysr.at[dy], (0, 0, 0, dy))

    def start_near(k):
        for side in range(2):
            for h in range(2):
                near(h, k, side).start()

    def take_near(k):
        for h in range(2):
            for side in range(2):
                near(h, k, side).wait_recv()
            pass_near(h, k).start()

    steps(0, 2)
    pl.semaphore_wait(bar, len(PEERS) + len(YPEERS))
    for h in range(2):
        far(h).start()
    sibling.start()
    steps(2, 4)
    start_near(0)
    for h in range(2):
        for q in range(4):
            cc_copy(h, q).start()
    steps(4, 7)
    c_copy(NCH - 1).wait()
    scores(NCH - 1, s1)
    first_pass(s0, m_ref, l_ref)
    first_pass(s1, m_ref, l_ref)

    m_t = jnp.transpose(m_ref[...])
    l_t = jnp.transpose(l_ref[...])
    top = jnp.max(m_t, axis=0, keepdims=True)
    total = jnp.sum(l_t * jnp.exp2((m_t - top) * SCALE), axis=0, keepdims=True)
    ystats[0, 0:8, :] = jnp.broadcast_to(top, (8, N))
    ystats[0, 8:16, :] = jnp.broadcast_to(total, (8, N))
    for dy in (1, 2, 3):
        ystat_copy(dy).start()
    for h in range(2):
        far(h).wait_recv()
    for dy in (1, 3, 2):
        y_send(0, dy).start()
    for h in range(2):
        for q in range(4):
            cc_copy(h, q).wait()
    for dy in (1, 2, 3):
        ystat_copy(dy).wait_recv()
    tops = [ystats[dy, 0:8, :] for dy in range(4)]
    top = functools.reduce(jnp.maximum, tops)
    total = sum(ystats[dy, 8:16, :] * jnp.exp2((tops[dy] - top) * SCALE) for dy in range(4))
    inv = 1.0 / total
    stats[0, 0, 0:8, :] = top
    stats[0, 0, 8:16, :] = inv
    stat_sibling().start()
    for h in range(2):
        for d in (1, 3, 2):
            stat_copy(h, d).start()

    def sums(h, rows_ref, top, inv):
        rows = rows_ref[...]
        for u in range(2):
            span = pl.ds(u * 256, 256)
            s = lax.dot_general(cc[h, span, :], rows, NT, preferred_element_type=F32)
            p = (jnp.exp2((s - top) * SCALE) * inv).astype(BF16)
            w = p.astype(F32)
            cols[h, span, :] += sum(w[:, g * 128 : (g + 1) * 128] for g in range(N // 128))
            acc[h, span, :] += lax.dot_general(p, rows, NN, preferred_element_type=F32)

    def chip_sums(rows, dc):
        for h in range(2):
            sums(h, rows, stats[dc, 0, 0:1, :], stats[dc, 0, 8:9, :])

    def near_sums(k, dc):
        lanes = pl.ds(k * PIECE, PIECE)
        for h in range(2):
            order = [slot(h, d) for d in (1, 3)]
            top = jnp.concatenate([stats[dc, i, 0:1, lanes] for i in order], axis=1)
            inv = jnp.concatenate([stats[dc, i, 8:9, lanes] for i in order], axis=1)
            sums(h, xn.at[h, k, pl.ds(dc * N, N)], top, inv)

    def far_sums(h, dc):
        k = slot(h, 2)
        sums(h, xf.at[h, dc], stats[dc, k, 0:1, :], stats[dc, k, 8:9, :])

    def take_far(h):
        for dy in (1, 3, 2):
            y_recv(h, dy).wait_recv()
        pass_far(h).start()

    def part(h, q):
        return remote(sb.at[h, q], rb.at[h, q], rs.at[h, q], rr.at[h, q], to_axis(1 - h, q))

    def weight(h, q):
        return remote(wsb.at[h, q], wrb.at[h, q], ws.at[h, q], wr.at[h, q], to_axis(1 - h, q))

    def tail(h, q):
        return jnp.sum(jnp.transpose(cols[h, pl.ds(q * HALF, HALF), :]), axis=0, keepdims=True)

    def send_parts(h):
        for q in (2, 1, 3):
            sb[h, q] = acc[h, pl.ds(q * HALF, HALF), :].astype(BF16)
            part(h, q).start()
        for q in (2, 1, 3):
            wsb[h, q] = jnp.broadcast_to(tail(h, q), (8, HALF))
            weight(h, q).start()

    def resp(a, b):
        @pl.loop(a, b)
        def _(j):
            for u in range(2):
                s = lax.dot_general(x_ref[...], cv[j, pl.ds(u * 256, 256), :], NT, preferred_element_type=F32)
                for g in range(2):
                    t = s[:, g * 128 : (g + 1) * 128]
                    lanes = pl.ds(pl.multiple_of(j * CH + u * 256 + g * 128, 128), 128)
                    resp_ref[:, lanes] = (jnp.exp2((t - topc[...]) * SCALE) * invc[...]).astype(BF16)

    chip_sums(x_ref, 0)
    for dy in (1, 3, 2):
        y_send(1, dy).start()
    start_near(1)
    sibling.wait_recv()
    stat_sibling().wait_recv()
    chip_sums(xs, 1)
    for h in range(2):
        for d in (1, 3, 2):
            stat_copy(h, d).wait_recv()
    stat_pass().start()
    topc[...] = jnp.transpose(jnp.broadcast_to(stats[0, 0, 0:1, :], (128, N)))
    invc[...] = jnp.transpose(jnp.broadcast_to(stats[0, 0, 8:9, :], (128, N)))
    take_near(0)
    near_sums(0, 0)
    stat_pass().wait_recv()
    for h in range(2):
        pass_near(h, 0).wait_recv()
    near_sums(0, 1)
    take_far(0)
    far_sums(0, 0)
    pass_far(0).wait_recv()
    far_sums(0, 1)
    sibling.wait_send()
    stat_sibling().wait_send()
    stat_pass().wait_send()
    for h in range(2):
        far(h).wait_send()
        pass_near(h, 0).wait_send()
        for side in range(2):
            near(h, 0, side).wait_send()
        for d in (1, 2, 3):
            stat_copy(h, d).wait_send()
    for dy in (1, 2, 3):
        ystat_copy(dy).wait_send()
        y_send(0, dy).wait_send()
    take_near(1)
    near_sums(1, 0)
    for h in range(2):
        pass_near(h, 1).wait_recv()
    near_sums(1, 1)
    take_far(1)
    send_parts(0)
    far_sums(1, 0)
    pass_far(1).wait_recv()
    far_sums(1, 1)
    send_parts(1)
    resp(0, NCH)
    for h in range(2):
        pass_near(h, 1).wait_send()
        for side in range(2):
            near(h, 1, side).wait_send()
        pass_far(h).wait_send()
    for dy in (1, 2, 3):
        y_send(1, dy).wait_send()

    for h in (0, 1):
        total = acc[h, 0:HALF, :]
        w = tail(h, 0)
        for q in (1, 3, 2):
            part(h, q).wait_recv()
            total = total + rb[h, q].astype(F32)
            weight(h, q).wait_recv()
            w = w + wrb[h, q, 0:1, :]
        numer_ref[pl.ds(h * HALF, HALF), :] = total
        w_ref[:, pl.ds(h * HALF, HALF)] = jnp.broadcast_to(w, (8, HALF))

    for h in range(2):
        for q in (1, 2, 3):
            part(h, q).wait_send()
            weight(h, q).wait_send()


def main_call(embeds, centroids):
    vmem = pl.BlockSpec(memory_space=pltpu.VMEM)
    dma = pltpu.SemaphoreType.DMA
    return pl.pallas_call(
        main_kernel,
        out_shape=[
            jax.ShapeDtypeStruct((N, KL), BF16),
            jax.ShapeDtypeStruct((OWN, D), F32),
            jax.ShapeDtypeStruct((8, OWN), F32),
        ],
        in_specs=[vmem, pl.BlockSpec(memory_space=pl.ANY)],
        out_specs=[vmem] * 3,
        scratch_shapes=[
            pltpu.VMEM((N, D), BF16),
            pltpu.VMEM((2, N // PIECE, 4 * PIECE, D), BF16),
            pltpu.VMEM((2, 2, N, D), BF16),
            pltpu.VMEM((NCH, CH, D), BF16),
            pltpu.VMEM((2, 4 * HALF, D), BF16),
            pltpu.VMEM((N, CH), F32),
            pltpu.VMEM((N, CH), F32),
            pltpu.VMEM((N, 128), F32),
            pltpu.VMEM((N, 128), F32),
            pltpu.VMEM((2, 4 * HALF, D), F32),
            pltpu.VMEM((2, 4 * HALF, 128), F32),
            pltpu.VMEM((2, 7, 16, N), F32),
            pltpu.VMEM((4, 16, N), F32),
            pltpu.VMEM((N, 128), F32),
            pltpu.VMEM((N, 128), F32),
            pltpu.VMEM((2, 4, HALF, D), BF16),
            pltpu.VMEM((2, 4, HALF, D), BF16),
            pltpu.VMEM((2, 4, 8, HALF), F32),
            pltpu.VMEM((2, 4, 8, HALF), F32),
            dma((NCH,)), dma((2, 4)), dma(()), dma(()),
            dma((2, 4, 2)), dma((2, 4, 2)), dma((2,)), dma((2,)), dma((2, 4)), dma((2, 4)),
            dma((2, 4)), dma((2, 4)), dma((2,)), dma((2,)), dma((8,)), dma((8,)), dma((4,)), dma((4,)),
            dma((2, 4)), dma((2, 4)), dma((2, 4)), dma((2, 4)),
        ],
        compiler_params=pltpu.CompilerParams(
            collective_id=0, has_side_effects=True, vmem_limit_bytes=VMEM_LIMIT
        ),
        cost_estimate=pl.CostEstimate(flops=26_000_000_000, bytes_accessed=22_000_000, transcendentals=13_000_000),
    )(embeds, centroids)


def out_kernel(resp_ref, numer_ref, w_ref, resp_out, numer_out, w_out, sem):
    copies = [
        pltpu.make_async_copy(resp_ref.at[pl.ds(i * 64, 64)], resp_out.at[pl.ds(i * 64, 64)], sem.at[i])
        for i in range(8)
    ]
    copies.append(pltpu.make_async_copy(numer_ref, numer_out, sem.at[8]))
    for copy in copies:
        copy.start()
    w_out[...] = w_ref[0:1, :]
    for copy in copies:
        copy.wait()


def out_call(resp, numer, weights):
    vmem, any_ = pl.BlockSpec(memory_space=pltpu.VMEM), pl.BlockSpec(memory_space=pl.ANY)
    return pl.pallas_call(
        out_kernel,
        out_shape=[
            jax.ShapeDtypeStruct((N, KL), BF16),
            jax.ShapeDtypeStruct((OWN, D), F32),
            jax.ShapeDtypeStruct((1, OWN), F32),
        ],
        in_specs=[vmem] * 3,
        out_specs=[any_, any_, vmem],
        scratch_shapes=[pltpu.SemaphoreType.DMA((9,))],
        compiler_params=pltpu.CompilerParams(vmem_limit_bytes=20 << 20),
    )(resp, numer, weights)


def shards(embeds, centroids):
    resp, numer, weights = out_call(*main_call(embeds, centroids))
    return resp, jnp.reshape(weights, (OWN,)), numer


def solution(mesh):
    return jax.shard_map(
        shards,
        mesh=mesh,
        in_specs=(P("rows", None), P("cent", None)),
        out_specs=(P("rows", "cent"), P(("cent", "rows")), P(("cent", "rows"), None)),
        check_vma=False,
    )
```

```python
import functools
import math

import jax
import jax.numpy as jnp
from jax import lax
from jax.experimental import pallas as pl
from jax.experimental.pallas import tpu as pltpu
from jax.sharding import PartitionSpec as P

N, D, KL = 512, 768, 8192
NZ = NX = NY = 4
CH = 512
AHEAD = 6
NCH = KL // CH
OWN = 256
QF = 128
PIECE = 256
HALF = 128
VMEM_LIMIT = 40 << 20
SCALE = 10.0 * math.log2(math.e)
F32, BF16 = jnp.float32, jnp.bfloat16
MESH = pl.DeviceIdType.MESH
NT = (((1,), (1,)), ((), ()))
NN = (((1,), (0,)), ((), ()))


def position():
    r = lax.axis_index("rows")
    y = lax.axis_index("cent")
    return lax.div(r, 8), lax.rem(lax.div(r, 2), 4), lax.rem(r, 2), y


def device(dz, dx, dc, dy):
    z, x, c, y = position()
    z, x, y = lax.rem(z + dz, 4), lax.rem(x + dx, 4), lax.rem(y + dy, 4)
    return ((z * 4 + x) * 2 + lax.rem(c + dc, 2), y)


def first_pass(s_ref, m_ref, l_ref):
    for t in range(N // 32):
        rows = pl.ds(t * 32, 32)
        s = [s_ref[rows, pl.ds(g * 128, 128)] for g in range(CH // 128)]
        m = m_ref[rows, :]
        top = functools.reduce(jnp.maximum, s, m)
        total = l_ref[rows, :] * jnp.exp2((m - top) * SCALE)
        for g in s:
            total = total + jnp.exp2((g - top) * SCALE)
        m_ref[rows, :] = top
        l_ref[rows, :] = total


def slot(h, d):
    return d + 3 * h if d else 0


def to_axis(h, d, dc=0):
    return (0, d, dc, 0) if h == 0 else (d, 0, dc, 0)


PEERS = [(0, 0, 1, 0)] + [to_axis(h, d) for h in range(2) for d in (1, 2, 3)]
YPEERS = [(0, 0, 0, dy) for dy in (1, 2, 3)]


def main_kernel(
    x_ref, c_hbm, resp_ref, numer_ref, w_ref,
    xs, xn, xf, cv, cc, s0, s1, m_ref, l_ref, acc, cols, stats, ystats, topc, invc, sb, rb, wsb, wrb,
    c_sem, cc_sem, own_s, own_r, near_s, near_r, far_s, far_r, ys, yr, pn_s, pn_r, pf_s, pf_r, ss, sr, yss, ysr, rs, rr, ws, wr,
):
    z, x, c, y = position()
    def c_copy(j):
        return pltpu.make_async_copy(c_hbm.at[pl.ds(j * CH, CH)], cv.at[j], c_sem.at[j])

    def cc_copy(h, q):
        owner = lax.rem(z + q, 4) * 8 + x * 2 + c if h == 0 else z * 8 + lax.rem(x + q, 4) * 2 + c
        start = pl.multiple_of(owner * OWN + h * HALF, HALF)
        return pltpu.make_async_copy(
            c_hbm.at[pl.ds(start, HALF)], cc.at[h, pl.ds(q * HALF, HALF)], cc_sem.at[h, q]
        )

    c_copy(0).start()
    bar = pltpu.get_barrier_semaphore()
    for p in PEERS + YPEERS:
        pl.semaphore_signal(bar, inc=1, device_id=device(*p), device_id_type=MESH)
    for j in range(1, AHEAD):
        c_copy(j).start()
    m_ref[...] = jnp.full(m_ref.shape, -3e38, F32)
    l_ref[...] = jnp.zeros(l_ref.shape, F32)
    acc[...] = jnp.zeros(acc.shape, F32)
    cols[...] = jnp.zeros(cols.shape, F32)

    def scores(j, out):
        out[...] = lax.dot_general(x_ref[...], cv[j], NT, preferred_element_type=F32)

    c_copy(0).wait()
    scores(0, s0)

    def steps(a, b):
        @pl.loop(a, b)
        def _(i):
            c_copy(2 * i + 1).wait()
            c_copy(2 * i + 2).wait()
            scores(2 * i + 1, s1)
            first_pass(s0, m_ref, l_ref)
            scores(2 * i + 2, s0)
            first_pass(s1, m_ref, l_ref)

            @pl.when(i < (NCH - AHEAD) // 2)
            def _():
                c_copy(2 * i + AHEAD).start()
                c_copy(2 * i + AHEAD + 1).start()

    def remote(src, dst, send, recv, to):
        return pltpu.make_async_remote_copy(
            src_ref=src, dst_ref=dst, send_sem=send, recv_sem=recv, device_id=device(*to), device_id_type=MESH
        )

    sibling = remote(x_ref, xs, own_s, own_r, (0, 0, 1, 0))

    def near(h, k, side):
        rows = pl.ds(side * PIECE, PIECE)
        return remote(
            x_ref.at[pl.ds(k * PIECE, PIECE)], xn.at[h, k, rows],
            near_s.at[h, k, side], near_r.at[h, k, side], to_axis(h, 3 if side == 0 else 1),
        )

    def pass_near(h, k):
        return remote(
            xn.at[h, k, pl.ds(0, 2 * PIECE)], xn.at[h, k, pl.ds(2 * PIECE, 2 * PIECE)],
            pn_s.at[h, k], pn_r.at[h, k], (0, 0, 1, 0),
        )

    def quarter(q):
        return pl.ds(pl.multiple_of(QF * q, QF), QF)

    def far(h):
        rows = quarter(y)
        return remote(x_ref.at[rows], xf.at[h, 0, rows], far_s.at[h], far_r.at[h], to_axis(h, 2))

    def y_send(h, dy):
        rows = xf.at[h, 0, quarter(y)]
        return remote(rows, rows, ys.at[h, dy], yr.at[h, dy], (0, 0, 0, dy))

    def y_recv(h, dy):
        rows = xf.at[h, 0, quarter(lax.rem(y + 4 - dy, 4))]
        return remote(rows, rows, ys.at[h, dy], yr.at[h, dy], (0, 0, 0, dy))

    def pass_far(h):
        return remote(xf.at[h, 0], xf.at[h, 1], pf_s.at[h], pf_r.at[h], (0, 0, 1, 0))

    def stat_copy(h, d):
        k = slot(h, d)
        return remote(stats.at[0, 0], stats.at[0, k], ss.at[k], sr.at[k], to_axis(h, 4 - d))

    def stat_sibling():
        return remote(stats.at[0, 0], stats.at[1, 0], ss.at[0], sr.at[0], (0, 0, 1, 0))

    def stat_pass():
        rows = pl.ds(1, 6)
        return remote(stats.at[0, rows], stats.at[1, rows], ss.at[7], sr.at[7], (0, 0, 1, 0))

    def ystat_copy(dy):
        return remote(ystats.at[0], ystats.at[dy], yss.at[dy], ysr.at[dy], (0, 0, 0, dy))

    def start_near(k):
        for side in range(2):
            for h in range(2):
                near(h, k, side).start()

    def take_near(k):
        for h in range(2):
            for side in range(2):
                near(h, k, side).wait_recv()
            pass_near(h, k).start()

    steps(0, 2)
    pl.semaphore_wait(bar, len(PEERS) + len(YPEERS))
    for h in range(2):
        far(h).start()
    sibling.start()
    steps(2, 4)
    start_near(0)
    for h in range(2):
        for q in range(4):
            cc_copy(h, q).start()
    steps(4, 7)
    c_copy(NCH - 1).wait()
    scores(NCH - 1, s1)
    first_pass(s0, m_ref, l_ref)
    first_pass(s1, m_ref, l_ref)

    m_t = jnp.transpose(m_ref[...])
    l_t = jnp.transpose(l_ref[...])
    top = jnp.max(m_t, axis=0, keepdims=True)
    total = jnp.sum(l_t * jnp.exp2((m_t - top) * SCALE), axis=0, keepdims=True)
    ystats[0, 0:8, :] = jnp.broadcast_to(top, (8, N))
    ystats[0, 8:16, :] = jnp.broadcast_to(total, (8, N))
    for dy in (1, 2, 3):
        ystat_copy(dy).start()
    for h in range(2):
        far(h).wait_recv()
    for dy in (1, 3, 2):
        y_send(0, dy).start()
    for h in range(2):
        for q in range(4):
            cc_copy(h, q).wait()
    for dy in (1, 2, 3):
        ystat_copy(dy).wait_recv()
    tops = [ystats[dy, 0:8, :] for dy in range(4)]
    top = functools.reduce(jnp.maximum, tops)
    total = sum(ystats[dy, 8:16, :] * jnp.exp2((tops[dy] - top) * SCALE) for dy in range(4))
    inv = 1.0 / total
    stats[0, 0, 0:8, :] = top
    stats[0, 0, 8:16, :] = inv
    stat_sibling().start()
    for h in range(2):
        for d in (1, 3, 2):
            stat_copy(h, d).start()

    def sums(h, rows_ref, top, inv):
        rows = rows_ref[...]
        for u in range(2):
            span = pl.ds(u * 256, 256)
            s = lax.dot_general(cc[h, span, :], rows, NT, preferred_element_type=F32)
            p = (jnp.exp2((s - top) * SCALE) * inv).astype(BF16)
            w = p.astype(F32)
            cols[h, span, :] += sum(w[:, g * 128 : (g + 1) * 128] for g in range(N // 128))
            acc[h, span, :] += lax.dot_general(p, rows, NN, preferred_element_type=F32)

    def chip_sums(rows, dc):
        for h in range(2):
            sums(h, rows, stats[dc, 0, 0:1, :], stats[dc, 0, 8:9, :])

    def near_sums(k, dc):
        lanes = pl.ds(k * PIECE, PIECE)
        for h in range(2):
            order = [slot(h, d) for d in (1, 3)]
            top = jnp.concatenate([stats[dc, i, 0:1, lanes] for i in order], axis=1)
            inv = jnp.concatenate([stats[dc, i, 8:9, lanes] for i in order], axis=1)
            sums(h, xn.at[h, k, pl.ds(dc * N, N)], top, inv)

    def far_sums(h, dc):
        k = slot(h, 2)
        sums(h, xf.at[h, dc], stats[dc, k, 0:1, :], stats[dc, k, 8:9, :])

    def take_far(h):
        for dy in (1, 3, 2):
            y_recv(h, dy).wait_recv()
        pass_far(h).start()

    def part(h, q):
        return remote(sb.at[h, q], rb.at[h, q], rs.at[h, q], rr.at[h, q], to_axis(1 - h, q))

    def weight(h, q):
        return remote(wsb.at[h, q], wrb.at[h, q], ws.at[h, q], wr.at[h, q], to_axis(1 - h, q))

    def tail(h, q):
        return jnp.sum(jnp.transpose(cols[h, pl.ds(q * HALF, HALF), :]), axis=0, keepdims=True)

    def send_parts(h):
        for q in (2, 1, 3):
            sb[h, q] = acc[h, pl.ds(q * HALF, HALF), :].astype(BF16)
            part(h, q).start()
        for q in (2, 1, 3):
            wsb[h, q] = jnp.broadcast_to(tail(h, q), (8, HALF))
            weight(h, q).start()

    def resp(a, b):
        @pl.loop(a, b, step=4)
        def _(first):
            for j, u in [(first + i, u) for i in range(4) for u in range(2)]:
                s = lax.dot_general(x_ref[...], cv[j, pl.ds(u * 256, 256), :], NT, preferred_element_type=F32)
                for g in range(2):
                    t = s[:, g * 128 : (g + 1) * 128]
                    lanes = pl.ds(pl.multiple_of(j * CH + u * 256 + g * 128, 128), 128)
                    resp_ref[:, lanes] = (jnp.exp2((t - topc[...]) * SCALE) * invc[...]).astype(BF16)

    chip_sums(x_ref, 0)
    for dy in (1, 3, 2):
        y_send(1, dy).start()
    start_near(1)
    sibling.wait_recv()
    stat_sibling().wait_recv()
    chip_sums(xs, 1)
    for h in range(2):
        for d in (1, 3, 2):
            stat_copy(h, d).wait_recv()
    stat_pass().start()
    topc[...] = jnp.transpose(jnp.broadcast_to(stats[0, 0, 0:1, :], (128, N)))
    invc[...] = jnp.transpose(jnp.broadcast_to(stats[0, 0, 8:9, :], (128, N)))
    take_near(0)
    near_sums(0, 0)
    stat_pass().wait_recv()
    for h in range(2):
        pass_near(h, 0).wait_recv()
    near_sums(0, 1)
    take_far(0)
    far_sums(0, 0)
    pass_far(0).wait_recv()
    far_sums(0, 1)
    sibling.wait_send()
    stat_sibling().wait_send()
    stat_pass().wait_send()
    for h in range(2):
        far(h).wait_send()
        pass_near(h, 0).wait_send()
        for side in range(2):
            near(h, 0, side).wait_send()
        for d in (1, 2, 3):
            stat_copy(h, d).wait_send()
    for dy in (1, 2, 3):
        ystat_copy(dy).wait_send()
        y_send(0, dy).wait_send()
    take_near(1)
    near_sums(1, 0)
    for h in range(2):
        pass_near(h, 1).wait_recv()
    near_sums(1, 1)
    take_far(1)
    send_parts(0)
    far_sums(1, 0)
    pass_far(1).wait_recv()
    far_sums(1, 1)
    send_parts(1)
    resp(0, NCH)
    for h in range(2):
        pass_near(h, 1).wait_send()
        for side in range(2):
            near(h, 1, side).wait_send()
        pass_far(h).wait_send()
    for dy in (1, 2, 3):
        y_send(1, dy).wait_send()

    for h in (0, 1):
        total = acc[h, 0:HALF, :]
        w = tail(h, 0)
        for q in (1, 3, 2):
            part(h, q).wait_recv()
            total = total + rb[h, q].astype(F32)
            weight(h, q).wait_recv()
            w = w + wrb[h, q, 0:1, :]
        numer_ref[pl.ds(h * HALF, HALF), :] = total
        w_ref[:, pl.ds(h * HALF, HALF)] = jnp.broadcast_to(w, (8, HALF))

    for h in range(2):
        for q in (1, 2, 3):
            part(h, q).wait_send()
            weight(h, q).wait_send()


def main_call(embeds, centroids):
    vmem = pl.BlockSpec(memory_space=pltpu.VMEM)
    dma = pltpu.SemaphoreType.DMA
    return pl.pallas_call(
        main_kernel,
        out_shape=[
            jax.ShapeDtypeStruct((N, KL), BF16),
            jax.ShapeDtypeStruct((OWN, D), F32),
            jax.ShapeDtypeStruct((8, OWN), F32),
        ],
        in_specs=[vmem, pl.BlockSpec(memory_space=pl.ANY)],
        out_specs=[vmem] * 3,
        scratch_shapes=[
            pltpu.VMEM((N, D), BF16),
            pltpu.VMEM((2, N // PIECE, 4 * PIECE, D), BF16),
            pltpu.VMEM((2, 2, N, D), BF16),
            pltpu.VMEM((NCH, CH, D), BF16),
            pltpu.VMEM((2, 4 * HALF, D), BF16),
            pltpu.VMEM((N, CH), F32),
            pltpu.VMEM((N, CH), F32),
            pltpu.VMEM((N, 128), F32),
            pltpu.VMEM((N, 128), F32),
            pltpu.VMEM((2, 4 * HALF, D), F32),
            pltpu.VMEM((2, 4 * HALF, 128), F32),
            pltpu.VMEM((2, 7, 16, N), F32),
            pltpu.VMEM((4, 16, N), F32),
            pltpu.VMEM((N, 128), F32),
            pltpu.VMEM((N, 128), F32),
            pltpu.VMEM((2, 4, HALF, D), BF16),
            pltpu.VMEM((2, 4, HALF, D), BF16),
            pltpu.VMEM((2, 4, 8, HALF), F32),
            pltpu.VMEM((2, 4, 8, HALF), F32),
            dma((NCH,)), dma((2, 4)), dma(()), dma(()),
            dma((2, 4, 2)), dma((2, 4, 2)), dma((2,)), dma((2,)), dma((2, 4)), dma((2, 4)),
            dma((2, 4)), dma((2, 4)), dma((2,)), dma((2,)), dma((8,)), dma((8,)), dma((4,)), dma((4,)),
            dma((2, 4)), dma((2, 4)), dma((2, 4)), dma((2, 4)),
        ],
        compiler_params=pltpu.CompilerParams(
            collective_id=0, has_side_effects=True, vmem_limit_bytes=VMEM_LIMIT
        ),
        cost_estimate=pl.CostEstimate(flops=26_000_000_000, bytes_accessed=22_000_000, transcendentals=13_000_000),
    )(embeds, centroids)


def out_kernel(resp_ref, numer_ref, w_ref, resp_out, numer_out, w_out, sem):
    copies = [
        pltpu.make_async_copy(resp_ref.at[pl.ds(i * 64, 64)], resp_out.at[pl.ds(i * 64, 64)], sem.at[i])
        for i in range(8)
    ]
    copies.append(pltpu.make_async_copy(numer_ref, numer_out, sem.at[8]))
    for copy in copies:
        copy.start()
    w_out[...] = w_ref[0:1, :]
    for copy in copies:
        copy.wait()


def out_call(resp, numer, weights):
    vmem, any_ = pl.BlockSpec(memory_space=pltpu.VMEM), pl.BlockSpec(memory_space=pl.ANY)
    return pl.pallas_call(
        out_kernel,
        out_shape=[
            jax.ShapeDtypeStruct((N, KL), BF16),
            jax.ShapeDtypeStruct((OWN, D), F32),
            jax.ShapeDtypeStruct((1, OWN), F32),
        ],
        in_specs=[vmem] * 3,
        out_specs=[any_, any_, vmem],
        scratch_shapes=[pltpu.SemaphoreType.DMA((9,))],
        compiler_params=pltpu.CompilerParams(vmem_limit_bytes=20 << 20),
    )(resp, numer, weights)


def shards(embeds, centroids):
    resp, numer, weights = out_call(*main_call(embeds, centroids))
    return resp, jnp.reshape(weights, (OWN,)), numer


def solution(mesh):
    return jax.shard_map(
        shards,
        mesh=mesh,
        in_specs=(P("rows", None), P("cent", None)),
        out_specs=(P("rows", "cent"), P(("cent", "rows")), P(("cent", "rows"), None)),
        check_vma=False,
    )
```

```python
import functools
import math

import jax
import jax.numpy as jnp
from jax import lax
from jax.experimental import pallas as pl
from jax.experimental.pallas import tpu as pltpu
from jax.sharding import PartitionSpec as P

N, D, KL = 512, 768, 8192
NZ = NX = NY = 4
CH = 512
AHEAD = 6
NCH = KL // CH
OWN = 256
QF = 128
PIECE = 256
HALF = 128
VMEM_LIMIT = 40 << 20
SCALE = 10.0 * math.log2(math.e)
F32, BF16 = jnp.float32, jnp.bfloat16
MESH = pl.DeviceIdType.MESH
NT = (((1,), (1,)), ((), ()))
NN = (((1,), (0,)), ((), ()))


def position():
    r = lax.axis_index("rows")
    y = lax.axis_index("cent")
    return lax.div(r, 8), lax.rem(lax.div(r, 2), 4), lax.rem(r, 2), y


def device(dz, dx, dc, dy):
    z, x, c, y = position()
    z, x, y = lax.rem(z + dz, 4), lax.rem(x + dx, 4), lax.rem(y + dy, 4)
    return ((z * 4 + x) * 2 + lax.rem(c + dc, 2), y)


def first_pass(s_ref, m_ref, l_ref):
    for t in range(N // 32):
        rows = pl.ds(t * 32, 32)
        s = [s_ref[rows, pl.ds(g * 128, 128)] for g in range(CH // 128)]
        m = m_ref[rows, :]
        top = functools.reduce(jnp.maximum, s, m)
        total = l_ref[rows, :] * jnp.exp2((m - top) * SCALE)
        for g in s:
            total = total + jnp.exp2((g - top) * SCALE)
        m_ref[rows, :] = top
        l_ref[rows, :] = total


def slot(h, d):
    return d + 3 * h if d else 0


def to_axis(h, d, dc=0):
    return (0, d, dc, 0) if h == 0 else (d, 0, dc, 0)


PEERS = [(0, 0, 1, 0)] + [to_axis(h, d) for h in range(2) for d in (1, 2, 3)]
YPEERS = [(0, 0, 0, dy) for dy in (1, 2, 3)]


def main_kernel(
    x_ref, c_hbm, resp_ref, numer_ref, w_ref,
    xs, xn, xf, cv, cc, s0, s1, m_ref, l_ref, acc, cols, stats, ystats, topc, invc, sb, rb, wsb, wrb,
    c_sem, cc_sem, own_s, own_r, near_s, near_r, far_s, far_r, ys, yr, pn_s, pn_r, pf_s, pf_r, ss, sr, yss, ysr, rs, rr, ws, wr,
):
    z, x, c, y = position()
    def c_copy(j):
        return pltpu.make_async_copy(c_hbm.at[pl.ds(j * CH, CH)], cv.at[j], c_sem.at[j])

    def cc_copy(h, q):
        owner = lax.rem(z + q, 4) * 8 + x * 2 + c if h == 0 else z * 8 + lax.rem(x + q, 4) * 2 + c
        start = pl.multiple_of(owner * OWN + h * HALF, HALF)
        return pltpu.make_async_copy(
            c_hbm.at[pl.ds(start, HALF)], cc.at[h, pl.ds(q * HALF, HALF)], cc_sem.at[h, q]
        )

    c_copy(0).start()
    bar = pltpu.get_barrier_semaphore()
    for p in PEERS + YPEERS:
        pl.semaphore_signal(bar, inc=1, device_id=device(*p), device_id_type=MESH)
    for j in range(1, AHEAD):
        c_copy(j).start()
    m_ref[...] = jnp.full(m_ref.shape, -3e38, F32)
    l_ref[...] = jnp.zeros(l_ref.shape, F32)
    acc[...] = jnp.zeros(acc.shape, F32)
    cols[...] = jnp.zeros(cols.shape, F32)

    def scores(j, out):
        out[...] = lax.dot_general(x_ref[...], cv[j], NT, preferred_element_type=F32)

    c_copy(0).wait()
    scores(0, s0)

    def steps(a, b):
        @pl.loop(a, b)
        def _(i):
            c_copy(2 * i + 1).wait()
            c_copy(2 * i + 2).wait()
            scores(2 * i + 1, s1)
            first_pass(s0, m_ref, l_ref)
            scores(2 * i + 2, s0)
            first_pass(s1, m_ref, l_ref)

            @pl.when(i < (NCH - AHEAD) // 2)
            def _():
                c_copy(2 * i + AHEAD).start()
                c_copy(2 * i + AHEAD + 1).start()

    def remote(src, dst, send, recv, to):
        return pltpu.make_async_remote_copy(
            src_ref=src, dst_ref=dst, send_sem=send, recv_sem=recv, device_id=device(*to), device_id_type=MESH
        )

    sibling = remote(x_ref, xs, own_s, own_r, (0, 0, 1, 0))

    def near(h, k, side):
        rows = pl.ds(side * PIECE, PIECE)
        return remote(
            x_ref.at[pl.ds(k * PIECE, PIECE)], xn.at[h, k, rows],
            near_s.at[h, k, side], near_r.at[h, k, side], to_axis(h, 3 if side == 0 else 1),
        )

    def pass_near(h, k):
        return remote(
            xn.at[h, k, pl.ds(0, 2 * PIECE)], xn.at[h, k, pl.ds(2 * PIECE, 2 * PIECE)],
            pn_s.at[h, k], pn_r.at[h, k], (0, 0, 1, 0),
        )

    def quarter(q):
        return pl.ds(pl.multiple_of(QF * q, QF), QF)

    def far(h):
        rows = quarter(y)
        return remote(x_ref.at[rows], xf.at[h, 0, rows], far_s.at[h], far_r.at[h], to_axis(h, 2))

    def y_send(h, dy):
        rows = xf.at[h, 0, quarter(y)]
        return remote(rows, rows, ys.at[h, dy], yr.at[h, dy], (0, 0, 0, dy))

    def y_recv(h, dy):
        rows = xf.at[h, 0, quarter(lax.rem(y + 4 - dy, 4))]
        return remote(rows, rows, ys.at[h, dy], yr.at[h, dy], (0, 0, 0, dy))

    def pass_far(h):
        return remote(xf.at[h, 0], xf.at[h, 1], pf_s.at[h], pf_r.at[h], (0, 0, 1, 0))

    def stat_copy(h, d):
        k = slot(h, d)
        return remote(stats.at[0, 0], stats.at[0, k], ss.at[k], sr.at[k], to_axis(h, 4 - d))

    def stat_sibling():
        return remote(stats.at[0, 0], stats.at[1, 0], ss.at[0], sr.at[0], (0, 0, 1, 0))

    def stat_pass():
        rows = pl.ds(1, 6)
        return remote(stats.at[0, rows], stats.at[1, rows], ss.at[7], sr.at[7], (0, 0, 1, 0))

    def ystat_copy(dy):
        return remote(ystats.at[0], ystats.at[dy], yss.at[dy], ysr.at[dy], (0, 0, 0, dy))

    def start_near(k):
        for side in range(2):
            for h in range(2):
                near(h, k, side).start()

    def take_near(k):
        for h in range(2):
            for side in range(2):
                near(h, k, side).wait_recv()
            pass_near(h, k).start()

    steps(0, 2)
    pl.semaphore_wait(bar, len(PEERS) + len(YPEERS))
    for h in range(2):
        far(h).start()
    sibling.start()
    steps(2, 4)
    start_near(0)
    for h in range(2):
        for q in range(4):
            cc_copy(h, q).start()
    steps(4, 7)
    c_copy(NCH - 1).wait()
    scores(NCH - 1, s1)
    first_pass(s0, m_ref, l_ref)
    first_pass(s1, m_ref, l_ref)

    m_t = jnp.transpose(m_ref[...])
    l_t = jnp.transpose(l_ref[...])
    top = jnp.max(m_t, axis=0, keepdims=True)
    total = jnp.sum(l_t * jnp.exp2((m_t - top) * SCALE), axis=0, keepdims=True)
    ystats[0, 0:8, :] = jnp.broadcast_to(top, (8, N))
    ystats[0, 8:16, :] = jnp.broadcast_to(total, (8, N))
    for dy in (1, 2, 3):
        ystat_copy(dy).start()
    for h in range(2):
        far(h).wait_recv()
    for dy in (1, 3, 2):
        y_send(0, dy).start()
    for h in range(2):
        for q in range(4):
            cc_copy(h, q).wait()
    for dy in (1, 2, 3):
        ystat_copy(dy).wait_recv()
    tops = [ystats[dy, 0:8, :] for dy in range(4)]
    top = functools.reduce(jnp.maximum, tops)
    total = sum(ystats[dy, 8:16, :] * jnp.exp2((tops[dy] - top) * SCALE) for dy in range(4))
    inv = 1.0 / total
    stats[0, 0, 0:8, :] = top
    stats[0, 0, 8:16, :] = inv
    stat_sibling().start()
    for h in range(2):
        for d in (1, 3, 2):
            stat_copy(h, d).start()

    def sums(h, rows_ref, top, inv, units=(0, 1)):
        rows = rows_ref[...]
        for u in units:
            span = pl.ds(u * 256, 256)
            s = lax.dot_general(cc[h, span, :], rows, NT, preferred_element_type=F32)
            p = (jnp.exp2((s - top) * SCALE) * inv).astype(BF16)
            w = p.astype(F32)
            cols[h, span, :] += sum(w[:, g * 128 : (g + 1) * 128] for g in range(N // 128))
            acc[h, span, :] += lax.dot_general(p, rows, NN, preferred_element_type=F32)

    def chip_sums(rows, dc):
        for h in range(2):
            sums(h, rows, stats[dc, 0, 0:1, :], stats[dc, 0, 8:9, :])

    def near_sums(k, dc):
        lanes = pl.ds(k * PIECE, PIECE)
        for h in range(2):
            order = [slot(h, d) for d in (1, 3)]
            top = jnp.concatenate([stats[dc, i, 0:1, lanes] for i in order], axis=1)
            inv = jnp.concatenate([stats[dc, i, 8:9, lanes] for i in order], axis=1)
            sums(h, xn.at[h, k, pl.ds(dc * N, N)], top, inv)

    def far_sums(h, dc, units=(0, 1)):
        k = slot(h, 2)
        sums(h, xf.at[h, dc], stats[dc, k, 0:1, :], stats[dc, k, 8:9, :], units)

    def take_far(h):
        for dy in (1, 3, 2):
            y_recv(h, dy).wait_recv()
        pass_far(h).start()

    def part(h, q):
        return remote(sb.at[h, q], rb.at[h, q], rs.at[h, q], rr.at[h, q], to_axis(1 - h, q))

    def weight(h, q):
        return remote(wsb.at[h, q], wrb.at[h, q], ws.at[h, q], wr.at[h, q], to_axis(1 - h, q))

    def tail(h, q):
        return jnp.sum(jnp.transpose(cols[h, pl.ds(q * HALF, HALF), :]), axis=0, keepdims=True)

    def send_parts(h, owners=(2, 1, 3)):
        for q in owners:
            sb[h, q] = acc[h, pl.ds(q * HALF, HALF), :].astype(BF16)
            part(h, q).start()
        for q in owners:
            wsb[h, q] = jnp.broadcast_to(tail(h, q), (8, HALF))
            weight(h, q).start()

    def resp(a, b):
        @pl.loop(a, b, step=4)
        def _(first):
            for j, u in [(first + i, u) for i in range(4) for u in range(2)]:
                s = lax.dot_general(x_ref[...], cv[j, pl.ds(u * 256, 256), :], NT, preferred_element_type=F32)
                for g in range(2):
                    t = s[:, g * 128 : (g + 1) * 128]
                    lanes = pl.ds(pl.multiple_of(j * CH + u * 256 + g * 128, 128), 128)
                    resp_ref[:, lanes] = (jnp.exp2((t - topc[...]) * SCALE) * invc[...]).astype(BF16)

    chip_sums(x_ref, 0)
    for dy in (1, 3, 2):
        y_send(1, dy).start()
    start_near(1)
    sibling.wait_recv()
    stat_sibling().wait_recv()
    chip_sums(xs, 1)
    for h in range(2):
        for d in (1, 3, 2):
            stat_copy(h, d).wait_recv()
    stat_pass().start()
    topc[...] = jnp.transpose(jnp.broadcast_to(stats[0, 0, 0:1, :], (128, N)))
    invc[...] = jnp.transpose(jnp.broadcast_to(stats[0, 0, 8:9, :], (128, N)))
    take_near(0)
    near_sums(0, 0)
    stat_pass().wait_recv()
    for h in range(2):
        pass_near(h, 0).wait_recv()
    near_sums(0, 1)
    take_far(0)
    far_sums(0, 0)
    pass_far(0).wait_recv()
    far_sums(0, 1)
    sibling.wait_send()
    stat_sibling().wait_send()
    stat_pass().wait_send()
    for h in range(2):
        far(h).wait_send()
        pass_near(h, 0).wait_send()
        for side in range(2):
            near(h, 0, side).wait_send()
        for d in (1, 2, 3):
            stat_copy(h, d).wait_send()
    for dy in (1, 2, 3):
        ystat_copy(dy).wait_send()
        y_send(0, dy).wait_send()
    take_near(1)
    near_sums(1, 0)
    for h in range(2):
        pass_near(h, 1).wait_recv()
    near_sums(1, 1)
    take_far(1)
    send_parts(0)
    far_sums(1, 0)
    pass_far(1).wait_recv()
    far_sums(1, 1, (1,))
    send_parts(1, (2, 3))
    far_sums(1, 1, (0,))
    send_parts(1, (1,))
    resp(0, NCH)
    for h in range(2):
        pass_near(h, 1).wait_send()
        for side in range(2):
            near(h, 1, side).wait_send()
        pass_far(h).wait_send()
    for dy in (1, 2, 3):
        y_send(1, dy).wait_send()

    for h in (0, 1):
        total = acc[h, 0:HALF, :]
        w = tail(h, 0)
        for q in (1, 3, 2):
            part(h, q).wait_recv()
            total = total + rb[h, q].astype(F32)
            weight(h, q).wait_recv()
            w = w + wrb[h, q, 0:1, :]
        numer_ref[pl.ds(h * HALF, HALF), :] = total
        w_ref[:, pl.ds(h * HALF, HALF)] = jnp.broadcast_to(w, (8, HALF))

    for h in range(2):
        for q in (1, 2, 3):
            part(h, q).wait_send()
            weight(h, q).wait_send()


def main_call(embeds, centroids):
    vmem = pl.BlockSpec(memory_space=pltpu.VMEM)
    dma = pltpu.SemaphoreType.DMA
    return pl.pallas_call(
        main_kernel,
        out_shape=[
            jax.ShapeDtypeStruct((N, KL), BF16),
            jax.ShapeDtypeStruct((OWN, D), F32),
            jax.ShapeDtypeStruct((8, OWN), F32),
        ],
        in_specs=[vmem, pl.BlockSpec(memory_space=pl.ANY)],
        out_specs=[vmem] * 3,
        scratch_shapes=[
            pltpu.VMEM((N, D), BF16),
            pltpu.VMEM((2, N // PIECE, 4 * PIECE, D), BF16),
            pltpu.VMEM((2, 2, N, D), BF16),
            pltpu.VMEM((NCH, CH, D), BF16),
            pltpu.VMEM((2, 4 * HALF, D), BF16),
            pltpu.VMEM((N, CH), F32),
            pltpu.VMEM((N, CH), F32),
            pltpu.VMEM((N, 128), F32),
            pltpu.VMEM((N, 128), F32),
            pltpu.VMEM((2, 4 * HALF, D), F32),
            pltpu.VMEM((2, 4 * HALF, 128), F32),
            pltpu.VMEM((2, 7, 16, N), F32),
            pltpu.VMEM((4, 16, N), F32),
            pltpu.VMEM((N, 128), F32),
            pltpu.VMEM((N, 128), F32),
            pltpu.VMEM((2, 4, HALF, D), BF16),
            pltpu.VMEM((2, 4, HALF, D), BF16),
            pltpu.VMEM((2, 4, 8, HALF), F32),
            pltpu.VMEM((2, 4, 8, HALF), F32),
            dma((NCH,)), dma((2, 4)), dma(()), dma(()),
            dma((2, 4, 2)), dma((2, 4, 2)), dma((2,)), dma((2,)), dma((2, 4)), dma((2, 4)),
            dma((2, 4)), dma((2, 4)), dma((2,)), dma((2,)), dma((8,)), dma((8,)), dma((4,)), dma((4,)),
            dma((2, 4)), dma((2, 4)), dma((2, 4)), dma((2, 4)),
        ],
        compiler_params=pltpu.CompilerParams(
            collective_id=0, has_side_effects=True, vmem_limit_bytes=VMEM_LIMIT
        ),
        cost_estimate=pl.CostEstimate(flops=26_000_000_000, bytes_accessed=22_000_000, transcendentals=13_000_000),
    )(embeds, centroids)


def out_kernel(resp_ref, numer_ref, w_ref, resp_out, numer_out, w_out, sem):
    copies = [
        pltpu.make_async_copy(resp_ref.at[pl.ds(i * 64, 64)], resp_out.at[pl.ds(i * 64, 64)], sem.at[i])
        for i in range(8)
    ]
    copies.append(pltpu.make_async_copy(numer_ref, numer_out, sem.at[8]))
    for copy in copies:
        copy.start()
    w_out[...] = w_ref[0:1, :]
    for copy in copies:
        copy.wait()


def out_call(resp, numer, weights):
    vmem, any_ = pl.BlockSpec(memory_space=pltpu.VMEM), pl.BlockSpec(memory_space=pl.ANY)
    return pl.pallas_call(
        out_kernel,
        out_shape=[
            jax.ShapeDtypeStruct((N, KL), BF16),
            jax.ShapeDtypeStruct((OWN, D), F32),
            jax.ShapeDtypeStruct((1, OWN), F32),
        ],
        in_specs=[vmem] * 3,
        out_specs=[any_, any_, vmem],
        scratch_shapes=[pltpu.SemaphoreType.DMA((9,))],
        compiler_params=pltpu.CompilerParams(vmem_limit_bytes=20 << 20),
    )(resp, numer, weights)


def shards(embeds, centroids):
    resp, numer, weights = out_call(*main_call(embeds, centroids))
    return resp, jnp.reshape(weights, (OWN,)), numer


def solution(mesh):
    return jax.shard_map(
        shards,
        mesh=mesh,
        in_specs=(P("rows", None), P("cent", None)),
        out_specs=(P("rows", "cent"), P(("cent", "rows")), P(("cent", "rows"), None)),
        check_vma=False,
    )
```
